32 devices in a mesh: tm: 8 (over y, x, core), ens: 4 (over z).
Axes of the slice: x: 2, y: 2, z: 4, core: 2. Of those that a mesh axis runs over, the one named last changes fastest.
Arguments:
- propagators: float32 [4, 8, 512, 512], P('ens', 'tm'), may hold values from -1 to 1, as said below
- weights: float32 [4], P('ens'), may hold values from 2 to 8
- target: float32 [512, 512], replicated, may hold values from -1 to 1, as said below
Outputs:
- gradient: float32 [512, 8, 512], P('ens', 'tm')
The draws below stay inside these ranges and needn't reach their ends.
Inputs may be any that keep to these rules, and one draw needn't show every extreme that they name: Every propagators[m, t] is an orthogonal 512 x 512 matrix up to float32 rounding. target is an orthogonal 512 x 512 matrix up to float32 rounding.
All inputs are finite; a program needn't handle non-finite values.
Results may differ from the reference program's by a relative error of at most 0.0003.
Values sent between devices are 32-bit elements; how exact they have to be, the bound alone decides.
No kernel may reach another device: no remote copies, remote signals or barrier semaphores. Data moves between devices by JAX's collectives and lax.ppermute only.
A program may use at most 128 MiB of HBM per device.

```python
import math
import jax
import jax.numpy as jnp
from jax import lax

R = 512
NT = 8
MEMBERS = 4


def cayley(seed_key, spread):
    gaussian = jax.random.normal(seed_key, (R, R), jnp.float32) * (spread / math.sqrt(2.0 * R))
    skew_part = gaussian - gaussian.T
    identity = jnp.eye(R, dtype=jnp.float32)
    return jnp.linalg.solve(identity - skew_part, identity + skew_part)


def draw_propagators(key, part):
    spread = 0.8
    how_many = MEMBERS * NT

    def single(slot_index):
        return cayley(jax.random.fold_in(key, slot_index), spread)
    matrices = lax.map(single, jnp.arange(how_many, dtype=jnp.int32))
    return matrices.reshape(MEMBERS, NT, R, R)


def draw_target(key, part):
    spread = 1.0
    return cayley(jax.random.fold_in(key, 7919), spread)


def level_of(key, dims, split, low, high):
    def one(axis_at, blocks):
        draws = jax.random.uniform(jax.random.fold_in(jax.random.fold_in(key, 6), axis_at), (blocks,), jnp.float32, low / len(split), high / len(split))
        return jnp.repeat(jnp.exp(draws), dims[axis_at] // blocks).reshape((-1,) + (1,) * (len(dims) - axis_at - 1))

    level = one(*split[0])
    for cut in split[1:]:
        level = level * one(*cut)
    return level


def setup_inputs(seed: int = 0) -> dict:
    splits = jax.random.split(jax.random.key(seed), 4)
    propagators = draw_propagators(jax.random.fold_in(splits[3], 71), 0)
    weights = jnp.clip(jnp.exp(math.log(8.0) - 1.3862944 * jax.random.uniform(splits[1], (MEMBERS,), jnp.float32) ** level_of(splits[1], (MEMBERS,), ((0, 4),), -0.2, 0.2)), 2.0, 8.0)
    target = draw_target(jax.random.fold_in(splits[3], 71), 0)
    return {"propagators": propagators, "weights": weights, "target": target}


highest = lax.Precision.HIGHEST

def reference(propagators, weights, target):
    identity = jnp.eye(R, dtype=jnp.float32)

    def member(running_sum, inputs):
        member_slices, weight = inputs

        def advance(running, factor):
            running = jnp.dot(factor.astype(jnp.float32), running.astype(jnp.float32), precision=highest, preferred_element_type=jnp.float32)
            return (running, running)
        final_product, stacked = lax.scan(advance, identity, member_slices)
        twisted = jnp.dot(target.T.astype(jnp.float32), final_product.astype(jnp.float32), precision=highest, preferred_element_type=jnp.float32)
        skew_part = weight * (twisted - twisted.T) * 0.5
        right_factor = jnp.einsum('ij,tkj->tik', skew_part, stacked, precision=highest)
        member_term = jnp.einsum('tik,tkj->itj', stacked, right_factor, precision=highest)
        return (running_sum + member_term, None)
    zeros_init = jnp.zeros((R, NT, R), jnp.float32)
    summed, _ = lax.scan(member, zeros_init, (propagators, weights))
    return summed
```

```python
import functools

import jax
import jax.numpy as jnp
from jax import lax
from jax.experimental import pallas as pl
from jax.experimental.pallas import tpu as pltpu
from jax.sharding import PartitionSpec as P

LANES = 128
f32, bf16 = jnp.float32, jnp.bfloat16


def split(x):
    high = x.astype(bf16)
    return high, (x - high.astype(f32)).astype(bf16)


def product(a, b):
    (ah, al), (bh, bl) = split(a), split(b)
    dot = functools.partial(jnp.dot, preferred_element_type=f32)
    return dot(ah, bh) + (dot(al, bh) + dot(ah, bl))


def bit(level):
    return lax.rem(lax.div(lax.axis_index("tm"), 1 << level), 2)


def call(kernel, outs, *operands, scratch=()):
    return pl.pallas_call(
        kernel,
        out_shape=[jax.ShapeDtypeStruct(s, f32) for s in outs],
        in_specs=[pl.BlockSpec(memory_space=pltpu.VMEM)] * len(operands),
        out_specs=[pl.BlockSpec(memory_space=pltpu.VMEM)] * len(outs),
        scratch_shapes=[pltpu.VMEM(s, f32) for s in scratch],
        compiler_params=pltpu.CompilerParams(vmem_limit_bytes=48 << 20),
    )(*operands)


def place(full, mine, other):
    half = mine.shape[0]
    core = bit(0)
    full[pl.ds(pl.multiple_of(core * half, half), half), :] = mine[...]
    full[pl.ds(pl.multiple_of((1 - core) * half, half), half), :] = other[...]


def pair_kernel(mine, other, own, send, left, right, lo, hi, whole):
    core, turned = bit(0), bit(1)
    half = send.shape[0]
    order = mine.shape[0]

    @pl.when(core == 0)
    def _():
        lo[...] = mine[...]
        hi[...] = other[...]

    @pl.when(core == 1)
    def _():
        lo[...] = other[...]
        hi[...] = mine[...]

    both = product(hi[...], lo[...])
    identity = (lax.broadcasted_iota(jnp.int32, (order, order), 0) == lax.broadcasted_iota(jnp.int32, (order, order), 1)).astype(f32)
    rows = pl.ds(pl.multiple_of(core * half, half), half)

    @pl.when(turned == 0)
    def _():
        own[...] = both
        whole[...] = both.T

    @pl.when(turned == 1)
    def _():
        own[...] = both.T
        whole[...] = both

    send[...] = whole[rows, :]

    @pl.when((core == 0) & (turned == 0))
    def _():
        left[...] = lo[...]
        right[...] = hi[...]

    @pl.when((core == 0) & (turned == 1))
    def _():
        left[...] = hi[...].T
        right[...] = lo[...].T

    @pl.when((core == 1) & (turned == 0))
    def _():
        left[...] = both
        right[...] = identity

    @pl.when((core == 1) & (turned == 1))
    def _():
        left[...] = identity
        right[...] = both.T


def turn_kernel(level, mine, other, left, right, got, got_other, own, send, left_out, right_out, full):
    core = bit(0)
    half = send.shape[0]
    flip = bit(level) != bit(level + 1)
    place(full, got, got_other)
    new_right = product(full[...], right[...])
    place(full, mine, other)

    @pl.when(flip)
    def _():
        own[...] = full[...].T
        left_out[...] = new_right.T
        right_out[...] = left[...].T

    @pl.when(jnp.logical_not(flip))
    def _():
        own[...] = full[...]
        full[...] = full[...].T
        left_out[...] = left[...]
        right_out[...] = new_right

    send[...] = full[pl.ds(pl.multiple_of(core * half, half), half), :]


def half_kernel(got, own, out):
    out[...] = product(got[...], own[...])


def factor_kernel(top, got, got_other, left, right, target, left_out, right_out, full):
    turned, later = bit(top - 1), bit(top)
    place(full, got, got_other)
    full[...] = product(full[...], right[...])
    left_out[...] = left[...]
    right_out[...] = full[...]

    @pl.when((later == 0) & (turned == 0))
    def _():
        left_out[...] = product(left[...], target[...].T)

    @pl.when((later == 0) & (turned == 1))
    def _():
        right_out[...] = product(target[...], full[...])

    @pl.when((later == 1) & (turned == 0))
    def _():
        right_out[...] = product(target[...].T, full[...])

    @pl.when((later == 1) & (turned == 1))
    def _():
        left_out[...] = product(left[...], target[...])


def gradient_kernel(top, mine, other, left, right, weight, *rest):
    blocks, (full, terms) = rest[:-2], rest[-2:]
    place(full, mine, other)
    turned = bit(top - 1)
    scale = weight[...] * (0.5 - turned.astype(f32))
    cyclic = product(product(left[...], full[...]), right[...])
    terms[...] = scale * (cyclic - cyclic.T)
    count = len(blocks)
    rows = terms.shape[0] // count
    spread = terms.shape[1] // LANES
    place_z = lax.axis_index("ens")
    for step, block in enumerate(blocks):
        which = lax.rem(place_z + step, count)
        part = terms[pl.ds(pl.multiple_of(which * rows, rows), rows), :]
        for j in range(spread):
            block[pl.ds(j, rows, stride=spread), :] = part[:, j * LANES:(j + 1) * LANES]


def sum_kernel(*refs):
    total = refs[0][...]
    for ref in refs[1:-1]:
        total = total + ref[...]
    refs[-1][...] = total


def shards(levels, members, propagators, weights, target):
    order = target.shape[0]
    half, square = (order // 2, order), (order, order)
    slices = 1 << levels

    def swap(x, level):
        return lax.ppermute(x, "tm", [(i, i ^ (1 << level)) for i in range(slices)])

    slice_here = propagators[0, 0]
    other = swap(slice_here, 0)
    own, send, left, right = call(pair_kernel, [square, half, square, square], slice_here, other, scratch=[square] * 3)
    top = levels - 1
    for level in range(1, top):
        got = swap(send, level)
        product_half = call(half_kernel, [half], got, own)[0]
        got_other = swap(got, 0)
        if level + 1 < top:
            own, send, left, right = call(
                functools.partial(turn_kernel, level), [square, half, square, square],
                product_half, swap(product_half, 0), left, right, got, got_other, scratch=[square])
    far = swap(product_half, top)
    left, right = call(functools.partial(factor_kernel, top), [square] * 2, got, got_other, left, right, target, scratch=[square])
    spread = order // LANES
    rows = order // members
    blocks = call(
        functools.partial(gradient_kernel, top), [(rows * spread, LANES)] * members,
        far, swap(far, 0), left, right, weights.reshape(1, 1), scratch=[square] * 2)
    arrived = [blocks[0]] + [
        lax.ppermute(blocks[s], "ens", [(i, (i + s) % members) for i in range(members)]) for s in range(1, members)]
    total = call(sum_kernel, [(rows * spread, LANES)], *arrived)[0]
    return total.reshape(rows, 1, order)


def solution(mesh):
    levels = mesh.shape["tm"].bit_length() - 1
    assert mesh.shape["tm"] == 1 << levels and levels >= 3
    placed = (P("ens", "tm", None, None), P("ens"), P())
    return jax.shard_map(
        functools.partial(shards, levels, mesh.shape["ens"]),
        mesh=mesh, in_specs=placed, out_specs=P("ens", "tm", None), check_vma=False)
```

```python
import functools

import jax
import jax.numpy as jnp
from jax import lax
from jax.experimental import pallas as pl
from jax.experimental.pallas import tpu as pltpu
from jax.sharding import PartitionSpec as P

LANES = 128
PIECES = (1, 1, 1, 1)
f32, bf16 = jnp.float32, jnp.bfloat16


def split(x):
    high = x.astype(bf16)
    return high, (x - high.astype(f32)).astype(bf16)


def product(a, b, b_turned=False):
    (ah, al), (bh, bl) = split(a), split(b)
    dims = (((1,), (1 if b_turned else 0,)), ((), ()))
    dot = functools.partial(lax.dot_general, dimension_numbers=dims, preferred_element_type=f32)
    return dot(ah, bh) + (dot(al, bh) + dot(ah, bl))


def bit(level):
    return lax.rem(lax.div(lax.axis_index("tm"), 1 << level), 2)


def call(kernel, outs, *operands, scratch=()):
    return pl.pallas_call(
        kernel,
        out_shape=[jax.ShapeDtypeStruct(s, f32) for s in outs],
        in_specs=[pl.BlockSpec(memory_space=pltpu.VMEM)] * len(operands),
        out_specs=[pl.BlockSpec(memory_space=pltpu.VMEM)] * len(outs),
        scratch_shapes=[pltpu.VMEM(s, f32) for s in scratch],
        compiler_params=pltpu.CompilerParams(vmem_limit_bytes=48 << 20),
    )(*operands)


def place(full, mine, other):
    half = full.shape[0] // 2
    core = bit(0)
    for pieces, base in ((mine, core * half), (other, (1 - core) * half)):
        at = 0
        for piece in pieces:
            rows = piece.shape[0]
            full[pl.ds(pl.multiple_of(base + at, 8), rows), :] = piece[...]
            at += rows


def cut(rows, pieces):
    at = 0
    for piece in pieces:
        piece[...] = rows[at:at + piece.shape[0], :]
        at += piece.shape[0]


def early_kernel(slice_here, target, mine):
    first = lax.axis_index("tm") == 0

    @pl.when(first)
    def _():
        mine[...] = product(slice_here[...], target[...], b_turned=True)

    @pl.when(jnp.logical_not(first))
    def _():
        mine[...] = slice_here[...]


def send_kernel(mine, other, target, *rest):
    sends, columns = rest[:-1], rest[-1]
    core, turned = bit(0), bit(1)
    half = mine.shape[0] // 2

    @pl.when((turned == 0) & (core == 0))
    def _():
        cut(product(other[...], mine[:, :half]).T, sends)

    @pl.when((turned == 0) & (core == 1))
    def _():
        columns[...] = other[:, half:]

        @pl.when(lax.axis_index("tm") == 1)
        def _():
            columns[...] = product(other[...], target[half:, :], b_turned=True)

        cut(product(mine[...], columns[...]).T, sends)

    @pl.when((turned == 1) & (core == 0))
    def _():
        cut(product(other[:half, :], mine[...]), sends)

    @pl.when((turned == 1) & (core == 1))
    def _():
        cut(product(mine[half:, :], other[...]), sends)


def own_kernel(mine, other, target, own, left, right, lo, hi):
    core, turned = bit(0), bit(1)
    order = mine.shape[0]

    @pl.when(core == 0)
    def _():
        lo[...] = mine[...]
        hi[...] = other[...]

    @pl.when(core == 1)
    def _():
        lo[...] = other[...]
        hi[...] = mine[...]

        @pl.when(lax.axis_index("tm") == 1)
        def _():
            lo[...] = product(other[...], target[...], b_turned=True)

    both = product(hi[...], lo[...])
    identity = (lax.broadcasted_iota(jnp.int32, (order, order), 0) == lax.broadcasted_iota(jnp.int32, (order, order), 1)).astype(f32)

    @pl.when(turned == 0)
    def _():
        own[...] = both

        @pl.when(core == 0)
        def _():
            left[...] = lo[...]
            right[...] = hi[...]

        @pl.when(core == 1)
        def _():
            left[...] = both
            right[...] = identity

    @pl.when(turned == 1)
    def _():
        over = both.T
        own[...] = over

        @pl.when(core == 0)
        def _():
            left[...] = hi[...].T
            right[...] = lo[...].T

        @pl.when(core == 1)
        def _():
            left[...] = identity
            right[...] = over


def turn_kernel(level, count, *refs):
    mine, other, got, got_other = (refs[i * count:(i + 1) * count] for i in range(4))
    left, right, own, left_out, right_out = refs[4 * count:4 * count + 5]
    sends, full = refs[4 * count + 5:-1], refs[-1]
    half = full.shape[0] // 2
    flip = bit(level) != bit(level + 1)
    place(full, got, got_other)
    new_right = product(full[...], right[...])
    place(full, mine, other)

    @pl.when(flip)
    def _():
        own[...] = full[...].T
        left_out[...] = new_right.T
        right_out[...] = left[...].T

    @pl.when(jnp.logical_not(flip))
    def _():
        own[...] = full[...]
        full[...] = full[...].T
        left_out[...] = left[...]
        right_out[...] = new_right

    cut(full[pl.ds(pl.multiple_of(bit(0) * half, 8), half), :], sends)


def half_kernel(got, own, out):
    out[...] = product(got[...], own[...])


def factor_kernel(count, *refs):
    right, out, full = refs[2 * count:]
    place(full, refs[:count], refs[count:2 * count])
    out[...] = product(full[...], right[...])


def gradient_kernel(turned_level, count, order_of, *refs):
    left, right, weight = refs[2 * count:2 * count + 3]
    blocks, (full, terms) = refs[2 * count + 3:-2], refs[-2:]
    place(full, refs[:count], refs[count:2 * count])
    scale = weight[...] * (0.5 - bit(turned_level).astype(f32))
    cyclic = product(left[...], product(full[...], right[...]))
    terms[...] = scale * (cyclic - cyclic.T)
    rows = terms.shape[0] // len(blocks)
    spread = terms.shape[1] // LANES
    here = lax.axis_index("ens")
    for step, block in enumerate(blocks):
        part = terms[pl.ds(pl.multiple_of(order_of(here, step) * rows, 8), rows), :]
        for j in range(spread):
            block[pl.ds(j, rows, stride=spread), :] = part[:, j * LANES:(j + 1) * LANES]


def sum_kernel(*refs):
    terms, out = refs[:-1], refs[-1]
    here = lax.axis_index("ens")
    total = terms[0][...]
    for term in terms[1:-1]:
        total = total + term[...]
    out[...] = total

    @pl.when((here == 0) | (here == 3))
    def _():
        out[...] = total + terms[-1][...]


def plain_sum_kernel(*refs):
    total = refs[0][...]
    for ref in refs[1:-1]:
        total = total + ref[...]
    refs[-1][...] = total


def reduce_rows(blocks, shape):
    members = len(blocks)

    def move(x, pairs):
        return lax.ppermute(x, "ens", pairs)

    if members == 4:
        over_two = move(blocks[2], [(0, 1), (1, 3), (3, 2), (2, 0)])
        across = move(blocks[3], [(0, 3), (3, 0)])
        beside = move(blocks[1], [(0, 1), (1, 0), (2, 3), (3, 2)])
        joined = move(blocks[3] + over_two, [(1, 2), (2, 1)])
        return call(sum_kernel, [shape], blocks[0], beside, across, joined, over_two)[0]
    arrived = [move(blocks[s], [(i, (i + s) % members) for i in range(members)]) for s in range(1, members)]
    return call(plain_sum_kernel, [shape], blocks[0], *arrived)[0]


def shards(levels, members, propagators, weights, target):
    order = target.shape[0]
    square = (order, order)
    slices = 1 << levels
    count = len(PIECES)
    pieces = [(order // 2 * p // sum(PIECES), order) for p in PIECES]

    def swap(x, level):
        return lax.ppermute(x, "tm", [(i, i ^ (1 << level)) for i in range(slices)])

    slice_here = propagators[0, 0]
    other = swap(slice_here, 0)
    mine = call(early_kernel, [square], slice_here, target)[0]
    sends = call(send_kernel, pieces, mine, other, target, scratch=[(order, order // 2)])
    own, left, right = call(own_kernel, [square] * 3, mine, other, target, scratch=[square] * 2)
    top = levels - 1
    for level in range(1, top):
        got = [swap(s, level) for s in sends]
        products = [call(half_kernel, [g.shape], g, own)[0] for g in got]
        got_other = [swap(g, 0) for g in got]
        if level + 1 < top:
            outs = call(
                functools.partial(turn_kernel, level, count), [square] * 3 + pieces,
                *products, *[swap(p, 0) for p in products], *got, *got_other, left, right, scratch=[square])
            (own, left, right), sends = outs[:3], outs[3:]
    far = [swap(p, top) for p in products]
    right = call(functools.partial(factor_kernel, count), [square], *got, *got_other, right, scratch=[square])[0]
    far_other = [swap(f, 0) for f in far]
    rows, spread = order // members, order // LANES
    block = (rows * spread, LANES)
    order_of = (lambda here, step: here ^ step) if members == 4 else (lambda here, step: lax.rem(here + step, members))
    blocks = call(
        functools.partial(gradient_kernel, top - 1, count, order_of), [block] * members,
        *far, *far_other, left, right, weights.reshape(1, 1), scratch=[square] * 2)
    return reduce_rows(blocks, block).reshape(rows, 1, order)


def solution(mesh):
    levels = mesh.shape["tm"].bit_length() - 1
    assert mesh.shape["tm"] == 1 << levels and levels >= 3
    placed = (P("ens", "tm", None, None), P("ens"), P())
    return jax.shard_map(
        functools.partial(shards, levels, mesh.shape["ens"]),
        mesh=mesh, in_specs=placed, out_specs=P("ens", "tm", None), check_vma=False)
```

```python
import functools

import jax
import jax.numpy as jnp
from jax import lax
from jax.experimental import pallas as pl
from jax.experimental.pallas import tpu as pltpu
from jax.sharding import PartitionSpec as P

LANES = 128
PIECES = (1, 1, 1, 1)
f32, bf16 = jnp.float32, jnp.bfloat16


def split(x):
    high = x.astype(bf16)
    return high, (x - high.astype(f32)).astype(bf16)


def product(a, b, b_turned=False):
    (ah, al), (bh, bl) = split(a), split(b)
    dims = (((1,), (1 if b_turned else 0,)), ((), ()))
    dot = functools.partial(lax.dot_general, dimension_numbers=dims, preferred_element_type=f32)
    return dot(ah, bh) + (dot(al, bh) + dot(ah, bl))


def bit(level):
    return lax.rem(lax.div(lax.axis_index("tm"), 1 << level), 2)


def call(kernel, outs, *operands, scratch=()):
    return pl.pallas_call(
        kernel,
        out_shape=[jax.ShapeDtypeStruct(s, f32) for s in outs],
        in_specs=[pl.BlockSpec(memory_space=pltpu.VMEM)] * len(operands),
        out_specs=[pl.BlockSpec(memory_space=pltpu.VMEM)] * len(outs),
        scratch_shapes=[pltpu.VMEM(s, f32) for s in scratch],
        compiler_params=pltpu.CompilerParams(vmem_limit_bytes=48 << 20),
    )(*operands)


def place(full, mine, other):
    half = full.shape[0] // 2
    core = bit(0)
    for pieces, base in ((mine, core * half), (other, (1 - core) * half)):
        at = 0
        for piece in pieces:
            rows = piece.shape[0]
            full[pl.ds(pl.multiple_of(base + at, 8), rows), :] = piece[...]
            at += rows


def cut(rows, pieces):
    at = 0
    for piece in pieces:
        piece[...] = rows[at:at + piece.shape[0], :]
        at += piece.shape[0]


def early_kernel(slice_here, target, mine, target_here, arrivals):
    copies = [
        pltpu.make_async_copy(slice_here, mine, arrivals.at[0]), pltpu.make_async_copy(target, target_here, arrivals.at[1])]
    for copy in copies:
        copy.start()
    for copy in copies:
        copy.wait()

    @pl.when(lax.axis_index("tm") == 0)
    def _():
        mine[...] = product(mine[...], target_here[...], b_turned=True)


def send_kernel(mine, other, target, *rest):
    sends, columns = rest[:-1], rest[-1]
    core, turned = bit(0), bit(1)
    half = mine.shape[0] // 2

    @pl.when((turned == 0) & (core == 0))
    def _():
        cut(product(other[...], mine[:, :half]).T, sends)

    @pl.when((turned == 0) & (core == 1))
    def _():
        columns[...] = other[:, half:]

        @pl.when(lax.axis_index("tm") == 1)
        def _():
            columns[...] = product(other[...], target[half:, :], b_turned=True)

        cut(product(mine[...], columns[...]).T, sends)

    @pl.when((turned == 1) & (core == 0))
    def _():
        cut(product(other[:half, :], mine[...]), sends)

    @pl.when((turned == 1) & (core == 1))
    def _():
        cut(product(mine[half:, :], other[...]), sends)


def own_kernel(mine, other, target, own, left, right, lo, hi):
    core, turned = bit(0), bit(1)
    order = mine.shape[0]

    @pl.when(core == 0)
    def _():
        lo[...] = mine[...]
        hi[...] = other[...]

    @pl.when(core == 1)
    def _():
        lo[...] = other[...]
        hi[...] = mine[...]

        @pl.when(lax.axis_index("tm") == 1)
        def _():
            lo[...] = product(other[...], target[...], b_turned=True)

    both = product(hi[...], lo[...])
    identity = (lax.broadcasted_iota(jnp.int32, (order, order), 0) == lax.broadcasted_iota(jnp.int32, (order, order), 1)).astype(f32)

    @pl.when(turned == 0)
    def _():
        own[...] = both

        @pl.when(core == 0)
        def _():
            left[...] = lo[...]
            right[...] = hi[...]

        @pl.when(core == 1)
        def _():
            left[...] = both
            right[...] = identity

    @pl.when(turned == 1)
    def _():
        over = both.T
        own[...] = over

        @pl.when(core == 0)
        def _():
            left[...] = hi[...].T
            right[...] = lo[...].T

        @pl.when(core == 1)
        def _():
            left[...] = identity
            right[...] = over


def turn_kernel(level, count, *refs):
    mine, other, got, got_other = (refs[i * count:(i + 1) * count] for i in range(4))
    left, right, own, left_out, right_out = refs[4 * count:4 * count + 5]
    sends, full = refs[4 * count + 5:-1], refs[-1]
    half = full.shape[0] // 2
    flip = bit(level) != bit(level + 1)
    place(full, got, got_other)
    new_right = product(full[...], right[...])
    place(full, mine, other)

    @pl.when(flip)
    def _():
        own[...] = full[...].T
        left_out[...] = new_right.T
        right_out[...] = left[...].T

    @pl.when(jnp.logical_not(flip))
    def _():
        own[...] = full[...]
        full[...] = full[...].T
        left_out[...] = left[...]
        right_out[...] = new_right

    cut(full[pl.ds(pl.multiple_of(bit(0) * half, 8), half), :], sends)


def half_kernel(got, own, out):
    out[...] = product(got[...], own[...])


def factor_kernel(count, *refs):
    right, out, full = refs[2 * count:]
    place(full, refs[:count], refs[count:2 * count])
    out[...] = product(full[...], right[...])


def corner(rows):
    return [lax.broadcasted_iota(jnp.int32, (rows // 2, rows), d) for d in (0, 1)]


def pack(square):
    rows = square.shape[0]
    half = rows // 2
    row, column = corner(rows)
    top, low = square[:half, :], pltpu.roll(square[half:, :], half, 1)
    return jnp.where((column >= half) | (column > row), top, jnp.where(column < row, low, 0.0))


def unpack(packed):
    half, rows = packed.shape
    row, column = corner(rows)
    over = jnp.concatenate([packed, jnp.zeros_like(packed)], 0).T
    top = jnp.where((column >= half) | (column > row), packed, jnp.where(column < row, -over[:half, :], 0.0))
    moved, over_moved = pltpu.roll(packed, half, 1), pltpu.roll(over[:half, :], half, 1)
    low = jnp.where(column - half < row, moved, jnp.where(column - half > row, -over_moved, 0.0))
    return jnp.concatenate([top, jnp.where(column < half, -over[half:, :], low)], 0)


def gradient_kernel(turned_level, count, order_of, packed, *refs):
    left, right, weight = refs[2 * count:2 * count + 3]
    blocks, (full, terms) = refs[2 * count + 3:-2], refs[-2:]
    place(full, refs[:count], refs[count:2 * count])
    scale = weight[...] * (0.5 - bit(turned_level).astype(f32))
    cyclic = product(left[...], product(full[...], right[...]))
    terms[...] = scale * (cyclic - cyclic.T)
    rows = terms.shape[0] // len(blocks)
    here = lax.axis_index("ens")
    for step, block in enumerate(blocks):
        which = order_of(here, step)
        at = pl.ds(pl.multiple_of(which * rows, 8), rows)
        if packed:
            for j in range(len(blocks) - 1):
                column = jnp.where(j < which, j, j + 1)
                block[j * rows:(j + 1) * rows, :] = terms[at, pl.ds(pl.multiple_of(column * rows, LANES), rows)]
            block[(len(blocks) - 1) * rows:, :] = pack(terms[at, pl.ds(pl.multiple_of(which * rows, LANES), rows)])
        else:
            for j in range(terms.shape[1] // LANES):
                block[j * rows:(j + 1) * rows, :] = terms[at, j * LANES:(j + 1) * LANES]


def sum_kernel(rows, packed, *refs):
    terms, (out, total) = refs[:-2], refs[-2:]
    spread = out.shape[0] // rows
    here = lax.axis_index("ens")
    added = terms[0][...]
    for term in terms[1:-1]:
        added = added + term[...]
    added = added + jnp.where((lax.axis_size("ens") != 4) | (here == 0) | (here == 3), terms[-1][...], 0.0)
    if packed:
        total[:(spread - 1) * rows, :] = added[:(spread - 1) * rows, :]
        total[(spread - 1) * rows:, :] = unpack(added[(spread - 1) * rows:, :])
    else:
        total[...] = added
    for j in range(spread):
        at = jnp.where(j < here, j, jnp.where(j == here, spread - 1, j - 1)) if packed else j
        out[pl.ds(j, rows, stride=spread), :] = total[pl.ds(pl.multiple_of(at * rows, 8), rows), :]


def send_rows(blocks):
    members = len(blocks)

    def move(x, pairs):
        return lax.ppermute(x, "ens", pairs)

    if members != 4:
        return [move(blocks[s], [(i, (i + s) % members) for i in range(members)]) for s in range(1, members)]
    _, beside, over_two, across = blocks
    over = move(over_two, [(0, 1), (1, 3), (3, 2), (2, 0)])
    arrived = [move(across, [(0, 3), (3, 0)]), move(beside, [(0, 1), (1, 0), (2, 3), (3, 2)])]
    return [*arrived, move(across + over, [(1, 2), (2, 1)]), over]


def shards(levels, members, propagators, weights, target):
    order = target.shape[0]
    square = (order, order)
    slices = 1 << levels
    count = len(PIECES)
    pieces = [(order // 2 * p // sum(PIECES), order) for p in PIECES]

    def swap(x, level):
        return lax.ppermute(x, "tm", [(i, i ^ (1 << level)) for i in range(slices)])

    slice_here = propagators[0, 0]
    other = swap(slice_here, 0)
    mine, target = pl.pallas_call(
        early_kernel,
        out_shape=[jax.ShapeDtypeStruct(square, f32)] * 2,
        in_specs=[pl.BlockSpec(memory_space=pltpu.HBM)] * 2,
        out_specs=[pl.BlockSpec(memory_space=pltpu.VMEM)] * 2,
        scratch_shapes=[pltpu.SemaphoreType.DMA((2,))],
        compiler_params=pltpu.CompilerParams(vmem_limit_bytes=48 << 20),
    )(slice_here, target)
    sends = call(send_kernel, pieces, mine, other, target, scratch=[(order, order // 2)])
    own, left, right = call(own_kernel, [square] * 3, mine, other, target, scratch=[square] * 2)
    top = levels - 1
    for level in range(1, top):
        got = [swap(s, level) for s in sends]
        products = [call(half_kernel, [g.shape], g, own)[0] for g in got]
        got_other = [swap(g, 0) for g in got]
        if level + 1 < top:
            outs = call(
                functools.partial(turn_kernel, level, count), [square] * 3 + pieces,
                *products, *[swap(p, 0) for p in products], *got, *got_other, left, right, scratch=[square])
            (own, left, right), sends = outs[:3], outs[3:]
    far = [swap(p, top) for p in products]
    right = call(functools.partial(factor_kernel, count), [square], *got, *got_other, right, scratch=[square])[0]
    far_other = [swap(f, 0) for f in far]
    rows, spread = order // members, order // LANES
    packed = rows == LANES
    block = (rows * spread - packed * rows // 2, LANES)
    order_of = (lambda here, step: here ^ step) if members == 4 else (lambda here, step: lax.rem(here + step, members))
    blocks = call(
        functools.partial(gradient_kernel, top - 1, count, order_of, packed),
        [block] * members, *far, *far_other, left, right, weights.reshape(1, 1), scratch=[square] * 2)
    arrived = send_rows(blocks)
    total = call(
        functools.partial(sum_kernel, rows, packed), [(rows * spread, LANES)], blocks[0], *arrived,
        scratch=[(rows * spread, LANES)])[0]
    return total.reshape(rows, 1, order)


def solution(mesh):
    levels = mesh.shape["tm"].bit_length() - 1
    assert mesh.shape["tm"] == 1 << levels and levels >= 3
    placed = (P("ens", "tm", None, None), P("ens"), P())
    return jax.shard_map(
        functools.partial(shards, levels, mesh.shape["ens"]),
        mesh=mesh, in_specs=placed, out_specs=P("ens", "tm", None), check_vma=False)
```

```python
import functools

import jax
import jax.numpy as jnp
from jax import lax
from jax.experimental import pallas as pl
from jax.experimental.pallas import tpu as pltpu
from jax.sharding import PartitionSpec as P

LANES = 128
PIECES = (1, 1, 1, 1)
f32, bf16 = jnp.float32, jnp.bfloat16


def split(x):
    high = x.astype(bf16)
    return high, (x - high.astype(f32)).astype(bf16)


def product(a, b, b_turned=False):
    (ah, al), (bh, bl) = split(a), split(b)
    dims = (((1,), (1 if b_turned else 0,)), ((), ()))
    dot = functools.partial(lax.dot_general, dimension_numbers=dims, preferred_element_type=f32)
    return dot(ah, bh) + (dot(al, bh) + dot(ah, bl))


def bit(level):
    return lax.rem(lax.div(lax.axis_index("tm"), 1 << level), 2)


def call(kernel, outs, *operands, scratch=()):
    return pl.pallas_call(
        kernel,
        out_shape=[jax.ShapeDtypeStruct(s, f32) for s in outs],
        in_specs=[pl.BlockSpec(memory_space=pltpu.VMEM)] * len(operands),
        out_specs=[pl.BlockSpec(memory_space=pltpu.VMEM)] * len(outs),
        scratch_shapes=[pltpu.VMEM(s, f32) for s in scratch],
        compiler_params=pltpu.CompilerParams(vmem_limit_bytes=16 << 20),
    )(*operands)


def place(full, mine, other):
    half = full.shape[0] // 2
    core = bit(0)
    for pieces, base in ((mine, core * half), (other, (1 - core) * half)):
        at = 0
        for piece in pieces:
            rows = piece.shape[0]
            full[pl.ds(pl.multiple_of(base + at, 8), rows), :] = piece[...]
            at += rows


def cut(rows, pieces):
    at = 0
    for piece in pieces:
        piece[...] = rows[at:at + piece.shape[0], :]
        at += piece.shape[0]


def early_kernel(slice_here, mine):
    mine[...] = slice_here[...]


def send_kernel(mine, other, *sends):
    core, turned = bit(0), bit(1)
    half = mine.shape[0] // 2

    @pl.when((turned == 0) & (core == 0))
    def _():
        cut(product(other[...], mine[:, :half]).T, sends)

    @pl.when((turned == 0) & (core == 1))
    def _():
        cut(product(mine[...], other[:, half:]).T, sends)

    @pl.when((turned == 1) & (core == 0))
    def _():
        cut(product(other[:half, :], mine[...]), sends)

    @pl.when((turned == 1) & (core == 1))
    def _():
        cut(product(mine[half:, :], other[...]), sends)


def own_kernel(short, mine, other, target, own, left, right):
    core, turned = bit(0), bit(1)
    takes = (bit(2) == turned) if short else (core < 0)

    def identity(out):
        row, column = (lax.broadcasted_iota(jnp.int32, out.shape, d) for d in (0, 1))
        out[...] = (row == column).astype(f32)

    @pl.when((core == 0) & (turned == 0))
    def _():
        left[...] = mine[...]
        right[...] = other[...]

        @pl.when(takes)
        def _():
            left[...] = product(left[...], target[...], b_turned=True)

        own[...] = product(other[...], left[...])

    @pl.when((core == 0) & (turned == 1))
    def _():
        left[...] = other[...].T
        right[...] = mine[...].T

        @pl.when(takes)
        def _():
            left[...] = product(left[...], target[...])

        own[...] = product(right[...], left[...])

    @pl.when((core == 1) & (turned == 0))
    def _():
        own[...] = product(mine[...], other[...])
        identity(right)

        @pl.when(takes)
        def _():
            own[...] = product(own[...], target[...], b_turned=True)

        left[...] = own[...]

    @pl.when((core == 1) & (turned == 1))
    def _():
        right[...] = product(mine[...], other[...]).T
        own[...] = right[...]
        identity(left)

        @pl.when(takes)
        def _():
            left[...] = target[...]
            own[...] = product(right[...], target[...])


def turn_kernel(top, level, count, *refs):
    mine, other, got, got_other = (refs[i * count:(i + 1) * count] for i in range(4))
    left, right, target, own, left_out, right_out = refs[4 * count:4 * count + 6]
    sends, full = refs[4 * count + 6:-1], refs[-1]
    half = full.shape[0] // 2
    flip = bit(level) != bit(level + 1)
    place(full, got, got_other)
    new_right = product(full[...], right[...])
    place(full, mine, other)

    @pl.when(flip)
    def _():
        own[...] = full[...].T
        left_out[...] = new_right.T
        right_out[...] = left[...].T

    @pl.when(jnp.logical_not(flip))
    def _():
        own[...] = full[...]
        full[...] = full[...].T
        left_out[...] = left[...]
        right_out[...] = new_right

    cut(full[pl.ds(pl.multiple_of(bit(0) * half, 8), half), :], sends)
    if level + 2 == top:
        for out in own, left_out:
            @pl.when((bit(top) == bit(level + 1)) & (bit(top) == 0))
            def _(out=out):
                out[...] = product(out[...], target[...], b_turned=True)

            @pl.when((bit(top) == bit(level + 1)) & (bit(top) == 1))
            def _(out=out):
                out[...] = product(out[...], target[...])


def half_kernel(got, own, out):
    out[...] = product(got[...], own[...])


def join_kernel(*refs):
    at = 0
    for piece in refs[:-1]:
        refs[-1][at:at + piece.shape[0], :] = piece[...]
        at += piece.shape[0]


def factor_kernel(near, near_other, right, out, full):
    place(full, [near], [near_other])
    out[...] = product(full[...], right[...])


def corner(rows):
    return [lax.broadcasted_iota(jnp.int32, (rows // 2, rows), d) for d in (0, 1)]


def pack(square):
    rows = square.shape[0]
    half = rows // 2
    row, column = corner(rows)
    top, low = square[:half, :], pltpu.roll(square[half:, :], half, 1)
    return jnp.where((column >= half) | (column > row), top, jnp.where(column < row, low, 0.0))


def unpack(packed):
    half, rows = packed.shape
    row, column = corner(rows)
    over = jnp.concatenate([packed, jnp.zeros_like(packed)], 0).T
    top = jnp.where((column >= half) | (column > row), packed, jnp.where(column < row, -over[:half, :], 0.0))
    moved, over_moved = pltpu.roll(packed, half, 1), pltpu.roll(over[:half, :], half, 1)
    low = jnp.where(column - half < row, moved, jnp.where(column - half > row, -over_moved, 0.0))
    return jnp.concatenate([top, jnp.where(column < half, -over[half:, :], low)], 0)


def gradient_kernel(turned_level, order_of, packed, far, far_other, left, right, weight, *refs):
    blocks, (full, terms) = refs[:-2], refs[-2:]
    place(full, [far], [far_other])
    scale = weight[...] * (0.5 - bit(turned_level).astype(f32))
    cyclic = product(left[...], product(full[...], right[...]))
    terms[...] = scale * (cyclic - cyclic.T)
    rows = terms.shape[0] // len(blocks)
    here = lax.axis_index("ens")
    for step, block in enumerate(blocks):
        which = order_of(here, step)
        at = pl.ds(pl.multiple_of(which * rows, 8), rows)
        if packed:
            for j in range(len(blocks) - 1):
                column = jnp.where(j < which, j, j + 1)
                block[j * rows:(j + 1) * rows, :] = terms[at, pl.ds(pl.multiple_of(column * rows, LANES), rows)]
            block[(len(blocks) - 1) * rows:, :] = pack(terms[at, pl.ds(pl.multiple_of(which * rows, LANES), rows)])
        else:
            for j in range(terms.shape[1] // LANES):
                block[j * rows:(j + 1) * rows, :] = terms[at, j * LANES:(j + 1) * LANES]


def sum_kernel(rows, packed, *refs):
    terms, (out, total) = refs[:-2], refs[-2:]
    spread = out.shape[0] // rows
    here = lax.axis_index("ens")
    added = terms[0][...]
    for term in terms[1:-1]:
        added = added + term[...]
    added = added + jnp.where((lax.axis_size("ens") != 4) | (here == 0) | (here == 3), terms[-1][...], 0.0)
    if packed:
        total[:(spread - 1) * rows, :] = added[:(spread - 1) * rows, :]
        total[(spread - 1) * rows:, :] = unpack(added[(spread - 1) * rows:, :])
    else:
        total[...] = added
    for j in range(spread):
        at = jnp.where(j < here, j, jnp.where(j == here, spread - 1, j - 1)) if packed else j
        out[pl.ds(j, rows, stride=spread), :] = total[pl.ds(pl.multiple_of(at * rows, 8), rows), :]


def send_rows(blocks):
    members = len(blocks)

    def move(x, pairs):
        return lax.ppermute(x, "ens", pairs)

    if members != 4:
        return [move(blocks[s], [(i, (i + s) % members) for i in range(members)]) for s in range(1, members)]
    _, beside, over_two, across = blocks
    over = move(over_two, [(0, 1), (1, 3), (3, 2), (2, 0)])
    arrived = [move(across, [(0, 3), (3, 0)]), move(beside, [(0, 1), (1, 0), (2, 3), (3, 2)])]
    return [*arrived, move(across + over, [(1, 2), (2, 1)]), over]


def shards(levels, members, propagators, weights, target):
    order = target.shape[0]
    square = (order, order)
    slices = 1 << levels
    count = len(PIECES)
    pieces = [(order // 2 * p // sum(PIECES), order) for p in PIECES]

    def swap(x, level):
        return lax.ppermute(x, "tm", [(i, i ^ (1 << level)) for i in range(slices)])

    slice_here = propagators[0, 0]
    other = swap(slice_here, 0)
    mine = call(early_kernel, [square], slice_here)[0]
    sends = call(send_kernel, pieces, mine, other)
    own, left, right = call(functools.partial(own_kernel, levels == 3), [square] * 3, mine, other, target)
    top = levels - 1
    for level in range(1, top):
        got = [swap(s, level) for s in sends]
        products = [call(half_kernel, [g.shape], g, own)[0] for g in got]
        if level + 1 < top:
            outs = call(
                functools.partial(turn_kernel, top, level, count), [square] * 3 + pieces, *products,
                *[swap(p, 0) for p in products], *got, *[swap(g, 0) for g in got], left, right, target, scratch=[square])
            (own, left, right), sends = outs[:3], outs[3:]
    far = [swap(p, top) for p in products]
    near = call(join_kernel, [(order // 2, order)], *got)[0]
    right = call(factor_kernel, [square], near, swap(near, 0), right, scratch=[square])[0]
    far = call(join_kernel, [(order // 2, order)], *far)[0]
    rows, spread = order // members, order // LANES
    packed = rows == LANES
    block = (rows * spread - packed * rows // 2, LANES)
    order_of = (lambda here, step: here ^ step) if members == 4 else (lambda here, step: lax.rem(here + step, members))
    blocks = call(
        functools.partial(gradient_kernel, top - 1, order_of, packed),
        [block] * members, far, swap(far, 0), left, right, weights.reshape(1, 1), scratch=[square] * 2)
    arrived = send_rows(blocks)
    total = call(
        functools.partial(sum_kernel, rows, packed), [(rows * spread, LANES)], blocks[0], *arrived,
        scratch=[(rows * spread, LANES)])[0]
    return total.reshape(rows, 1, order)


def solution(mesh):
    levels = mesh.shape["tm"].bit_length() - 1
    assert mesh.shape["tm"] == 1 << levels and levels >= 3
    placed = (P("ens", "tm", None, None), P("ens"), P())
    return jax.shard_map(
        functools.partial(shards, levels, mesh.shape["ens"]),
        mesh=mesh, in_specs=placed, out_specs=P("ens", "tm", None), check_vma=False)
```

```python
import functools

import jax
import jax.numpy as jnp
from jax import lax
from jax.experimental import pallas as pl
from jax.experimental.pallas import tpu as pltpu
from jax.sharding import PartitionSpec as P

LANES = 128
PIECES = (1, 1, 1, 1)
f32, bf16 = jnp.float32, jnp.bfloat16


def split(x):
    high = x.astype(bf16)
    return high, (x - high.astype(f32)).astype(bf16)


def product(a, b, b_turned=False):
    (ah, al), (bh, bl) = split(a), split(b)
    dims = (((1,), (1 if b_turned else 0,)), ((), ()))
    dot = functools.partial(lax.dot_general, dimension_numbers=dims, preferred_element_type=f32)
    return dot(ah, bh) + (dot(al, bh) + dot(ah, bl))


def bit(level):
    return lax.rem(lax.div(lax.axis_index("tm"), 1 << level), 2)


def call(kernel, outs, *operands, scratch=()):
    return pl.pallas_call(
        kernel,
        out_shape=[jax.ShapeDtypeStruct(s, f32) for s in outs],
        in_specs=[pl.BlockSpec(memory_space=pltpu.VMEM)] * len(operands),
        out_specs=[pl.BlockSpec(memory_space=pltpu.VMEM)] * len(outs),
        scratch_shapes=[pltpu.VMEM(s, f32) for s in scratch],
        compiler_params=pltpu.CompilerParams(vmem_limit_bytes=16 << 20),
    )(*operands)


def place(full, mine, other):
    half = full.shape[0] // 2
    core = bit(0)
    for pieces, base in ((mine, core * half), (other, (1 - core) * half)):
        at = 0
        for piece in pieces:
            rows = piece.shape[0]
            full[pl.ds(pl.multiple_of(base + at, 8), rows), :] = piece[...]
            at += rows


def cut(rows, pieces):
    at = 0
    for piece in pieces:
        piece[...] = rows[at:at + piece.shape[0], :]
        at += piece.shape[0]


def early_kernel(slice_here, mine):
    mine[...] = slice_here[...]


def send_kernel(mine, other, *sends):
    core, turned = bit(0), bit(1)
    half = mine.shape[0] // 2

    @pl.when((turned == 0) & (core == 0))
    def _():
        cut(product(other[...], mine[:, :half]).T, sends)

    @pl.when((turned == 0) & (core == 1))
    def _():
        cut(product(mine[...], other[:, half:]).T, sends)

    @pl.when((turned == 1) & (core == 0))
    def _():
        cut(product(other[:half, :], mine[...]), sends)

    @pl.when((turned == 1) & (core == 1))
    def _():
        cut(product(mine[half:, :], other[...]), sends)


def own_kernel(short, mine, other, target, own, left, right):
    core, turned = bit(0), bit(1)
    takes = (bit(2) == turned) if short else (core < 0)

    def identity(out):
        row, column = (lax.broadcasted_iota(jnp.int32, out.shape, d) for d in (0, 1))
        out[...] = (row == column).astype(f32)

    @pl.when((core == 0) & (turned == 0))
    def _():
        left[...] = mine[...]
        right[...] = other[...]

        @pl.when(takes)
        def _():
            left[...] = product(left[...], target[...], b_turned=True)

        own[...] = product(other[...], left[...])

    @pl.when((core == 0) & (turned == 1))
    def _():
        left[...] = other[...].T
        right[...] = mine[...].T

        @pl.when(takes)
        def _():
            left[...] = product(left[...], target[...])

        own[...] = product(right[...], left[...])

    @pl.when((core == 1) & (turned == 0))
    def _():
        own[...] = product(mine[...], other[...])
        identity(right)

        @pl.when(takes)
        def _():
            own[...] = product(own[...], target[...], b_turned=True)

        left[...] = own[...]

    @pl.when((core == 1) & (turned == 1))
    def _():
        right[...] = product(mine[...], other[...]).T
        own[...] = right[...]
        identity(left)

        @pl.when(takes)
        def _():
            left[...] = target[...]
            own[...] = product(right[...], target[...])


def turn_kernel(top, level, count, *refs):
    mine, other, got, got_other = (refs[i * count:(i + 1) * count] for i in range(4))
    left, right, target, own, left_out, right_out = refs[4 * count:4 * count + 6]
    sends, full = refs[4 * count + 6:-1], refs[-1]
    half = full.shape[0] // 2
    flip = bit(level) != bit(level + 1)
    place(full, got, got_other)
    new_right = product(full[...], right[...])
    place(full, mine, other)

    @pl.when(flip)
    def _():
        own[...] = full[...].T
        left_out[...] = new_right.T
        right_out[...] = left[...].T

    @pl.when(jnp.logical_not(flip))
    def _():
        own[...] = full[...]
        full[...] = full[...].T
        left_out[...] = left[...]
        right_out[...] = new_right

    cut(full[pl.ds(pl.multiple_of(bit(0) * half, 8), half), :], sends)
    if level + 2 == top:
        for out in own, left_out:
            @pl.when((bit(top) == bit(level + 1)) & (bit(top) == 0))
            def _(out=out):
                out[...] = product(out[...], target[...], b_turned=True)

            @pl.when((bit(top) == bit(level + 1)) & (bit(top) == 1))
            def _(out=out):
                out[...] = product(out[...], target[...])


def half_kernel(got, own, out):
    out[...] = product(got[...], own[...])


def join_kernel(*refs):
    at = 0
    for piece in refs[:-1]:
        refs[-1][at:at + piece.shape[0], :] = piece[...]
        at += piece.shape[0]


def factor_kernel(near, near_other, right, out, full):
    place(full, [near], [near_other])
    out[...] = product(full[...], right[...])


def corner(rows):
    return [lax.broadcasted_iota(jnp.int32, (rows // 2, rows), d) for d in (0, 1)]


def pack(square):
    rows = square.shape[0]
    half = rows // 2
    row, column = corner(rows)
    top, low = square[:half, :], pltpu.roll(square[half:, :], half, 1)
    return jnp.where((column >= half) | (column > row), top, jnp.where(column < row, low, 0.0))


def unpack(packed):
    half, rows = packed.shape
    row, column = corner(rows)
    over = jnp.concatenate([packed, jnp.zeros_like(packed)], 0).T
    top = jnp.where((column >= half) | (column > row), packed, jnp.where(column < row, -over[:half, :], 0.0))
    moved, over_moved = pltpu.roll(packed, half, 1), pltpu.roll(over[:half, :], half, 1)
    low = jnp.where(column - half < row, moved, jnp.where(column - half > row, -over_moved, 0.0))
    return jnp.concatenate([top, jnp.where(column < half, -over[half:, :], low)], 0)


def lay_out(block, part, which, packed):
    rows, columns = part.shape
    if not packed:
        for j in range(columns // LANES):
            block[j * rows:(j + 1) * rows, :] = part[:, j * LANES:(j + 1) * LANES]
        return
    count = columns // rows
    for j in range(count - 1):
        at = jnp.where(j < which, j, j + 1)
        block[j * rows:(j + 1) * rows, :] = part[:, pl.ds(pl.multiple_of(at * rows, LANES), rows)]
    block[(count - 1) * rows:, :] = pack(part[:, pl.ds(pl.multiple_of(which * rows, LANES), rows)])


def sign(turned_level, weight):
    return weight[...] * (0.5 - bit(turned_level).astype(f32))


def first_block_kernel(turned_level, which_of, far, far_other, left, right, weight, cyclic, block, full, part):
    place(full, [far], [far_other])
    cyclic[...] = product(left[...], product(full[...], right[...]))
    rows = part.shape[0]
    which = which_of(lax.axis_index("ens"))
    at = pl.ds(pl.multiple_of(which * rows, LANES), rows)
    part[...] = sign(turned_level, weight) * (cyclic[at, :] - cyclic[:, at].T)
    lay_out(block, part, which, True)


def blocks_kernel(turned_level, which_of, packed, cyclic, weight, *refs):
    blocks, terms = refs[:-1], refs[-1]
    terms[...] = sign(turned_level, weight) * (cyclic[...] - cyclic[...].T)
    rows = terms.shape[0] // lax.axis_size("ens")
    here = lax.axis_index("ens")
    for which, block in zip(which_of(here), blocks):
        lay_out(block, terms.at[pl.ds(pl.multiple_of(which * rows, 8), rows), :], which, packed)


def cyclic_kernel(far, far_other, left, right, cyclic, full):
    place(full, [far], [far_other])
    cyclic[...] = product(left[...], product(full[...], right[...]))


def sum_kernel(rows, packed, *refs):
    terms, (out, total) = refs[:-2], refs[-2:]
    spread = out.shape[0] // rows
    here = lax.axis_index("ens")
    added = terms[0][...]
    for term in terms[1:-1]:
        added = added + term[...]
    added = added + jnp.where((lax.axis_size("ens") != 4) | (here == 0) | (here == 3), terms[-1][...], 0.0)
    if packed:
        total[:(spread - 1) * rows, :] = added[:(spread - 1) * rows, :]
        total[(spread - 1) * rows:, :] = unpack(added[(spread - 1) * rows:, :])
    else:
        total[...] = added
    for j in range(spread):
        at = jnp.where(j < here, j, jnp.where(j == here, spread - 1, j - 1)) if packed else j
        out[pl.ds(j, rows, stride=spread), :] = total[pl.ds(pl.multiple_of(at * rows, 8), rows), :]


def send_rows(blocks):
    members = len(blocks)

    def move(x, pairs):
        return lax.ppermute(x, "ens", pairs)

    if members != 4:
        return [move(blocks[s], [(i, (i + s) % members) for i in range(members)]) for s in range(1, members)]
    _, beside, over_two, across = blocks
    over = move(over_two, [(0, 1), (1, 3), (3, 2), (2, 0)])
    arrived = [move(across, [(0, 3), (3, 0)]), move(beside, [(0, 1), (1, 0), (2, 3), (3, 2)])]
    return [*arrived, move(across + over, [(1, 2), (2, 1)]), over]


def shards(levels, members, propagators, weights, target):
    order = target.shape[0]
    square = (order, order)
    slices = 1 << levels
    count = len(PIECES)
    pieces = [(order // 2 * p // sum(PIECES), order) for p in PIECES]

    def swap(x, level):
        return lax.ppermute(x, "tm", [(i, i ^ (1 << level)) for i in range(slices)])

    slice_here = propagators[0, 0]
    other = swap(slice_here, 0)
    mine = call(early_kernel, [square], slice_here)[0]
    sends = call(send_kernel, pieces, mine, other)
    own, left, right = call(functools.partial(own_kernel, levels == 3), [square] * 3, mine, other, target)
    top = levels - 1
    for level in range(1, top):
        got = [swap(s, level) for s in sends]
        products = [call(half_kernel, [g.shape], g, own)[0] for g in got]
        if level + 1 < top:
            outs = call(
                functools.partial(turn_kernel, top, level, count), [square] * 3 + pieces, *products,
                *[swap(p, 0) for p in products], *got, *[swap(g, 0) for g in got], left, right, target, scratch=[square])
            (own, left, right), sends = outs[:3], outs[3:]
    far = [swap(p, top) for p in products]
    near = call(join_kernel, [(order // 2, order)], *got)[0]
    right = call(factor_kernel, [square], near, swap(near, 0), right, scratch=[square])[0]
    far = call(join_kernel, [(order // 2, order)], *far)[0]
    rows, spread = order // members, order // LANES
    packed = rows == LANES
    block = (rows * spread - packed * rows // 2, LANES)
    factors = (far, swap(far, 0), left, right, weights.reshape(1, 1))
    if members == 4 and packed:
        cyclic, over_two = call(
            functools.partial(first_block_kernel, top - 1, lambda here: here ^ 2), [square, block], *factors,
            scratch=[square, (rows, order)])
        blocks = call(
            functools.partial(blocks_kernel, top - 1, lambda here: (here, here ^ 1, here ^ 3), packed), [block] * 3,
            cyclic, factors[-1], scratch=[square])
        blocks = [blocks[0], blocks[1], over_two, blocks[2]]
    else:
        order_of = (lambda here: [here ^ s for s in range(members)]) if members == 4 else (
            lambda here: [lax.rem(here + s, members) for s in range(members)])
        cyclic = call(cyclic_kernel, [square], *factors[:4], scratch=[square])[0]
        blocks = call(
            functools.partial(blocks_kernel, top - 1, order_of, packed), [block] * members, cyclic, factors[-1],
            scratch=[square])
    arrived = send_rows(blocks)
    total = call(
        functools.partial(sum_kernel, rows, packed), [(rows * spread, LANES)], blocks[0], *arrived,
        scratch=[(rows * spread, LANES)])[0]
    return total.reshape(rows, 1, order)


def solution(mesh):
    levels = mesh.shape["tm"].bit_length() - 1
    assert mesh.shape["tm"] == 1 << levels and levels >= 3
    placed = (P("ens", "tm", None, None), P("ens"), P())
    return jax.shard_map(
        functools.partial(shards, levels, mesh.shape["ens"]),
        mesh=mesh, in_specs=placed, out_specs=P("ens", "tm", None), check_vma=False)
```

```python
import functools

import jax
import jax.numpy as jnp
from jax import lax
from jax.experimental import pallas as pl
from jax.experimental.pallas import tpu as pltpu
from jax.sharding import PartitionSpec as P

LANES = 128
PIECES = (1, 1, 1, 1)
f32, bf16 = jnp.float32, jnp.bfloat16


def split(x):
    high = x.astype(bf16)
    return high, (x - high.astype(f32)).astype(bf16)


def product(a, b, b_turned=False):
    (ah, al), (bh, bl) = split(a), split(b)
    dims = (((1,), (1 if b_turned else 0,)), ((), ()))
    dot = functools.partial(lax.dot_general, dimension_numbers=dims, preferred_element_type=f32)
    return dot(ah, bh) + (dot(al, bh) + dot(ah, bl))


def bit(level):
    return lax.rem(lax.div(lax.axis_index("tm"), 1 << level), 2)


def call(kernel, outs, *operands, scratch=()):
    return pl.pallas_call(
        kernel,
        out_shape=[jax.ShapeDtypeStruct(s, f32) for s in outs],
        in_specs=[pl.BlockSpec(memory_space=pltpu.VMEM)] * len(operands),
        out_specs=[pl.BlockSpec(memory_space=pltpu.VMEM)] * len(outs),
        scratch_shapes=[pltpu.VMEM(s, f32) for s in scratch],
        compiler_params=pltpu.CompilerParams(vmem_limit_bytes=16 << 20),
    )(*operands)


def place(full, mine, other):
    half = full.shape[0] // 2
    core = bit(0)
    for pieces, base in ((mine, core * half), (other, (1 - core) * half)):
        at = 0
        for piece in pieces:
            rows = piece.shape[0]
            full[pl.ds(pl.multiple_of(base + at, 8), rows), :] = piece[...]
            at += rows


def cut(rows, pieces):
    at = 0
    for piece in pieces:
        piece[...] = rows[at:at + piece.shape[0], :]
        at += piece.shape[0]


def early_kernel(slice_here, mine):
    mine[...] = slice_here[...]


def send_kernel(mine, other, *sends):
    core, turned = bit(0), bit(1)
    half = mine.shape[0] // 2

    @pl.when((turned == 0) & (core == 0))
    def _():
        cut(product(other[...], mine[:, :half]).T, sends)

    @pl.when((turned == 0) & (core == 1))
    def _():
        cut(product(mine[...], other[:, half:]).T, sends)

    @pl.when((turned == 1) & (core == 0))
    def _():
        cut(product(other[:half, :], mine[...]), sends)

    @pl.when((turned == 1) & (core == 1))
    def _():
        cut(product(mine[half:, :], other[...]), sends)


def own_kernel(short, mine, other, target, own, left, right):
    core, turned = bit(0), bit(1)
    takes = (bit(2) == turned) if short else (core < 0)

    def identity(out):
        row, column = (lax.broadcasted_iota(jnp.int32, out.shape, d) for d in (0, 1))
        out[...] = (row == column).astype(f32)

    @pl.when((core == 0) & (turned == 0))
    def _():
        left[...] = mine[...]
        right[...] = other[...]

        @pl.when(takes)
        def _():
            left[...] = product(left[...], target[...], b_turned=True)

        own[...] = product(other[...], left[...])

    @pl.when((core == 0) & (turned == 1))
    def _():
        left[...] = other[...].T
        right[...] = mine[...].T

        @pl.when(takes)
        def _():
            left[...] = product(left[...], target[...])

        own[...] = product(right[...], left[...])

    @pl.when((core == 1) & (turned == 0))
    def _():
        own[...] = product(mine[...], other[...])
        identity(right)

        @pl.when(takes)
        def _():
            own[...] = product(own[...], target[...], b_turned=True)

        left[...] = own[...]

    @pl.when((core == 1) & (turned == 1))
    def _():
        right[...] = product(mine[...], other[...]).T
        own[...] = right[...]
        identity(left)

        @pl.when(takes)
        def _():
            left[...] = target[...]
            own[...] = product(right[...], target[...])


def turn_kernel(top, level, count, *refs):
    mine, other, got, got_other = (refs[i * count:(i + 1) * count] for i in range(4))
    left, right, target, own, left_out, right_out = refs[4 * count:4 * count + 6]
    sends, full = refs[4 * count + 6:-1], refs[-1]
    half = full.shape[0] // 2
    flip = bit(level) != bit(level + 1)
    place(full, got, got_other)
    new_right = product(full[...], right[...])
    place(full, mine, other)

    @pl.when(flip)
    def _():
        own[...] = full[...].T
        left_out[...] = new_right.T
        right_out[...] = left[...].T

    @pl.when(jnp.logical_not(flip))
    def _():
        own[...] = full[...]
        full[...] = full[...].T
        left_out[...] = left[...]
        right_out[...] = new_right

    cut(full[pl.ds(pl.multiple_of(bit(0) * half, 8), half), :], sends)
    if level + 2 == top:
        for out in own, left_out:
            @pl.when((bit(top) == bit(level + 1)) & (bit(top) == 0))
            def _(out=out):
                out[...] = product(out[...], target[...], b_turned=True)

            @pl.when((bit(top) == bit(level + 1)) & (bit(top) == 1))
            def _(out=out):
                out[...] = product(out[...], target[...])


def half_kernel(got, own, out):
    out[...] = product(got[...], own[...])


def join_kernel(*refs):
    at = 0
    for piece in refs[:-1]:
        refs[-1][at:at + piece.shape[0], :] = piece[...]
        at += piece.shape[0]


def factor_kernel(near, near_other, right, out, full):
    place(full, [near], [near_other])
    out[...] = product(full[...], right[...])


def corner(rows):
    return [lax.broadcasted_iota(jnp.int32, (rows // 2, rows), d) for d in (0, 1)]


def pack(square):
    rows = square.shape[0]
    half = rows // 2
    row, column = corner(rows)
    top, low = square[:half, :], pltpu.roll(square[half:, :], half, 1)
    return jnp.where((column >= half) | (column > row), top, jnp.where(column < row, low, 0.0))


def unpack(packed):
    half, rows = packed.shape
    row, column = corner(rows)
    over = jnp.concatenate([packed, jnp.zeros_like(packed)], 0).T
    top = jnp.where((column >= half) | (column > row), packed, jnp.where(column < row, -over[:half, :], 0.0))
    moved, over_moved = pltpu.roll(packed, half, 1), pltpu.roll(over[:half, :], half, 1)
    low = jnp.where(column - half < row, moved, jnp.where(column - half > row, -over_moved, 0.0))
    return jnp.concatenate([top, jnp.where(column < half, -over[half:, :], low)], 0)


def lay_out(block, part, which, packed):
    rows, columns = part.shape
    if not packed:
        for j in range(columns // LANES):
            block[j * rows:(j + 1) * rows, :] = part[:, j * LANES:(j + 1) * LANES]
        return
    count = columns // rows
    for j in range(count - 1):
        at = jnp.where(j < which, j, j + 1)
        block[j * rows:(j + 1) * rows, :] = part[:, pl.ds(pl.multiple_of(at * rows, LANES), rows)]
    block[(count - 1) * rows:, :] = pack(part[:, pl.ds(pl.multiple_of(which * rows, LANES), rows)])


def sign(turned_level, weight):
    return weight[...] * (0.5 - bit(turned_level).astype(f32))


def first_block_kernel(turned_level, which_of, far, far_other, left, right, weight, half_way, block, full, columns):
    place(full, [far], [far_other])
    half_way[...] = product(full[...], right[...])
    rows = columns.shape[0]
    which = which_of(lax.axis_index("ens"))
    at = pl.ds(pl.multiple_of(which * rows, LANES), rows)
    full[...] = product(left[...], half_way[...])
    columns[...] = sign(turned_level, weight) * (full[at, :] - full[:, at].T)
    lay_out(block, columns, which, True)


def blocks_kernel(turned_level, which_of, packed, half_way, left, weight, *refs):
    blocks, terms = refs[:-1], refs[-1]
    cyclic = product(left[...], half_way[...])
    terms[...] = sign(turned_level, weight) * (cyclic - cyclic.T)
    rows = terms.shape[0] // lax.axis_size("ens")
    here = lax.axis_index("ens")
    for which, block in zip(which_of(here), blocks):
        lay_out(block, terms.at[pl.ds(pl.multiple_of(which * rows, 8), rows), :], which, packed)


def skew_block(turned_level, which, half_way, left, weight, block, columns):
    rows = columns.shape[0]
    at = pl.ds(pl.multiple_of(which * rows, LANES), rows)
    across = product(left[...], half_way[:, at]).T
    columns[...] = sign(turned_level, weight) * (product(left[at, :], half_way[...]) - across)
    lay_out(block, columns, which, True)


def later_blocks_kernel(turned_level, which_of, half_way, left, weight, own, *refs):
    blocks_kernel(turned_level, which_of, True, half_way, left, weight, *refs[:-1])
    skew_block(turned_level, lax.axis_index("ens"), half_way, left, weight, own, refs[-1])


def half_way_kernel(far, far_other, right, half_way, full):
    place(full, [far], [far_other])
    half_way[...] = product(full[...], right[...])


def sum_kernel(rows, packed, *refs):
    terms, (out, total) = refs[:-2], refs[-2:]
    spread = out.shape[0] // rows
    here = lax.axis_index("ens")
    added = terms[0][...]
    for term in terms[1:-1]:
        added = added + term[...]
    added = added + jnp.where((lax.axis_size("ens") != 4) | (here == 0) | (here == 3), terms[-1][...], 0.0)
    if packed:
        total[:(spread - 1) * rows, :] = added[:(spread - 1) * rows, :]
        total[(spread - 1) * rows:, :] = unpack(added[(spread - 1) * rows:, :])
    else:
        total[...] = added
    for j in range(spread):
        at = jnp.where(j < here, j, jnp.where(j == here, spread - 1, j - 1)) if packed else j
        out[pl.ds(j, rows, stride=spread), :] = total[pl.ds(pl.multiple_of(at * rows, 8), rows), :]


def send_rows(blocks):
    members = len(blocks)

    def move(x, pairs):
        return lax.ppermute(x, "ens", pairs)

    if members != 4:
        return [move(blocks[s], [(i, (i + s) % members) for i in range(members)]) for s in range(1, members)]
    _, beside, over_two, across = blocks
    over = move(over_two, [(0, 1), (1, 3), (3, 2), (2, 0)])
    arrived = [move(across, [(0, 3), (3, 0)]), move(beside, [(0, 1), (1, 0), (2, 3), (3, 2)])]
    return [*arrived, move(across + over, [(1, 2), (2, 1)]), over]


def shards(levels, members, propagators, weights, target):
    order = target.shape[0]
    square = (order, order)
    slices = 1 << levels
    count = len(PIECES)
    pieces = [(order // 2 * p // sum(PIECES), order) for p in PIECES]

    def swap(x, level):
        return lax.ppermute(x, "tm", [(i, i ^ (1 << level)) for i in range(slices)])

    slice_here = propagators[0, 0]
    other = swap(slice_here, 0)
    mine = call(early_kernel, [square], slice_here)[0]
    sends = call(send_kernel, pieces, mine, other)
    own, left, right = call(functools.partial(own_kernel, levels == 3), [square] * 3, mine, other, target)
    top = levels - 1
    for level in range(1, top):
        got = [swap(s, level) for s in sends]
        products = [call(half_kernel, [g.shape], g, own)[0] for g in got]
        if level + 1 < top:
            outs = call(
                functools.partial(turn_kernel, top, level, count), [square] * 3 + pieces, *products,
                *[swap(p, 0) for p in products], *got, *[swap(g, 0) for g in got], left, right, target, scratch=[square])
            (own, left, right), sends = outs[:3], outs[3:]
    far = [swap(p, top) for p in products]
    near = call(join_kernel, [(order // 2, order)], *got)[0]
    right = call(factor_kernel, [square], near, swap(near, 0), right, scratch=[square])[0]
    far = call(join_kernel, [(order // 2, order)], *far)[0]
    rows, spread = order // members, order // LANES
    packed = rows == LANES
    block = (rows * spread - packed * rows // 2, LANES)
    factors = (far, swap(far, 0), left, right, weights.reshape(1, 1))
    if members == 4 and packed:
        half_way, over_two = call(
            functools.partial(first_block_kernel, top - 1, lambda here: here ^ 2), [square, block], *factors,
            scratch=[square, (rows, order)])
        blocks = call(
            functools.partial(later_blocks_kernel, top - 1, lambda here: (here ^ 1, here ^ 3)), [block] * 3,
            half_way, left, factors[-1], scratch=[square, (rows, order)])
        blocks = [blocks[0], blocks[1], over_two, blocks[2]]
    else:
        order_of = (lambda here: [here ^ s for s in range(members)]) if members == 4 else (
            lambda here: [lax.rem(here + s, members) for s in range(members)])
        half_way = call(half_way_kernel, [square], *factors[:2], right, scratch=[square])[0]
        blocks = call(
            functools.partial(blocks_kernel, top - 1, order_of, packed), [block] * members, half_way, left, factors[-1],
            scratch=[square])
    arrived = send_rows(blocks)
    total = call(
        functools.partial(sum_kernel, rows, packed), [(rows * spread, LANES)], blocks[0], *arrived,
        scratch=[(rows * spread, LANES)])[0]
    return total.reshape(rows, 1, order)


def solution(mesh):
    levels = mesh.shape["tm"].bit_length() - 1
    assert mesh.shape["tm"] == 1 << levels and levels >= 3
    placed = (P("ens", "tm", None, None), P("ens"), P())
    return jax.shard_map(
        functools.partial(shards, levels, mesh.shape["ens"]),
        mesh=mesh, in_specs=placed, out_specs=P("ens", "tm", None), check_vma=False)
```

```python
import functools

import jax
import jax.numpy as jnp
from jax import lax
from jax.experimental import pallas as pl
from jax.experimental.pallas import tpu as pltpu
from jax.sharding import PartitionSpec as P

LANES = 128
PIECES = (1, 1, 1, 1)
f32, bf16 = jnp.float32, jnp.bfloat16


def split(x):
    high = x.astype(bf16)
    return high, (x - high.astype(f32)).astype(bf16)


def product(a, b, b_turned=False):
    return product_of(split(a), split(b), b_turned)


def product_of(a, b, b_turned=False):
    (ah, al), (bh, bl) = a, b
    dims = (((1,), (1 if b_turned else 0,)), ((), ()))
    dot = functools.partial(lax.dot_general, dimension_numbers=dims, preferred_element_type=f32)
    return dot(ah, bh) + (dot(al, bh) + dot(ah, bl))


def bit(level):
    return lax.rem(lax.div(lax.axis_index("tm"), 1 << level), 2)


def call(kernel, outs, *operands, scratch=()):
    return pl.pallas_call(
        kernel,
        out_shape=[jax.ShapeDtypeStruct(s, f32) if isinstance(s[0], int) else jax.ShapeDtypeStruct(*s) for s in outs],
        in_specs=[pl.BlockSpec(memory_space=pltpu.VMEM)] * len(operands),
        out_specs=[pl.BlockSpec(memory_space=pltpu.VMEM)] * len(outs),
        scratch_shapes=[pltpu.VMEM(s, f32) for s in scratch],
        compiler_params=pltpu.CompilerParams(vmem_limit_bytes=16 << 20),
    )(*operands)


def place(full, mine, other):
    half = full.shape[0] // 2
    core = bit(0)
    for pieces, base in ((mine, core * half), (other, (1 - core) * half)):
        at = 0
        for piece in pieces:
            rows = piece.shape[0]
            full[pl.ds(pl.multiple_of(base + at, 8), rows), :] = piece[...]
            at += rows


def cut(rows, pieces):
    at = 0
    for piece in pieces:
        piece[...] = rows[at:at + piece.shape[0], :]
        at += piece.shape[0]


def early_kernel(slice_here, mine):
    mine[...] = slice_here[...]


def send_kernel(mine, other, *sends):
    core, turned = bit(0), bit(1)
    half = mine.shape[0] // 2

    @pl.when((turned == 0) & (core == 0))
    def _():
        cut(product(other[...], mine[:, :half]).T, sends)

    @pl.when((turned == 0) & (core == 1))
    def _():
        cut(product(mine[...], other[:, half:]).T, sends)

    @pl.when((turned == 1) & (core == 0))
    def _():
        cut(product(other[:half, :], mine[...]), sends)

    @pl.when((turned == 1) & (core == 1))
    def _():
        cut(product(mine[half:, :], other[...]), sends)


def own_kernel(short, mine, other, target, own, left, right):
    core, turned = bit(0), bit(1)
    takes = (bit(2) == turned) if short else (core < 0)

    def identity(out):
        row, column = (lax.broadcasted_iota(jnp.int32, out.shape, d) for d in (0, 1))
        out[...] = (row == column).astype(f32)

    @pl.when((core == 0) & (turned == 0))
    def _():
        left[...] = mine[...]
        right[...] = other[...]

        @pl.when(takes)
        def _():
            left[...] = product(left[...], target[...], b_turned=True)

        own[...] = product(other[...], left[...])

    @pl.when((core == 0) & (turned == 1))
    def _():
        left[...] = other[...].T
        right[...] = mine[...].T

        @pl.when(takes)
        def _():
            left[...] = product(left[...], target[...])

        own[...] = product(right[...], left[...])

    @pl.when((core == 1) & (turned == 0))
    def _():
        own[...] = product(mine[...], other[...])
        identity(right)

        @pl.when(takes)
        def _():
            own[...] = product(own[...], target[...], b_turned=True)

        left[...] = own[...]

    @pl.when((core == 1) & (turned == 1))
    def _():
        right[...] = product(mine[...], other[...]).T
        own[...] = right[...]
        identity(left)

        @pl.when(takes)
        def _():
            left[...] = target[...]
            own[...] = product(right[...], target[...])


def turn_kernel(top, level, count, *refs):
    mine, other, got, got_other = (refs[i * count:(i + 1) * count] for i in range(4))
    left, right, target, own, left_out, right_out = refs[4 * count:4 * count + 6]
    sends, full = refs[4 * count + 6:-1], refs[-1]
    half = full.shape[0] // 2
    flip = bit(level) != bit(level + 1)
    place(full, got, got_other)
    new_right = product(full[...], right[...])
    place(full, mine, other)

    @pl.when(flip)
    def _():
        own[...] = full[...].T
        left_out[...] = new_right.T
        right_out[...] = left[...].T

    @pl.when(jnp.logical_not(flip))
    def _():
        own[...] = full[...]
        full[...] = full[...].T
        left_out[...] = left[...]
        right_out[...] = new_right

    cut(full[pl.ds(pl.multiple_of(bit(0) * half, 8), half), :], sends)
    if level + 2 == top:
        for out in own, left_out:
            @pl.when((bit(top) == bit(level + 1)) & (bit(top) == 0))
            def _(out=out):
                out[...] = product(out[...], target[...], b_turned=True)

            @pl.when((bit(top) == bit(level + 1)) & (bit(top) == 1))
            def _(out=out):
                out[...] = product(out[...], target[...])


def half_kernel(got, own, out):
    out[...] = product(got[...], own[...])


def join_kernel(*refs):
    at = 0
    for piece in refs[:-1]:
        refs[-1][at:at + piece.shape[0], :] = piece[...]
        at += piece.shape[0]


def factor_kernel(near, near_other, right, high, low, full):
    place(full, [near], [near_other])
    high[...], low[...] = split(product(full[...], right[...]))


def corner(rows):
    return [lax.broadcasted_iota(jnp.int32, (rows // 2, rows), d) for d in (0, 1)]


def pack(square):
    rows = square.shape[0]
    half = rows // 2
    row, column = corner(rows)
    top, low = square[:half, :], pltpu.roll(square[half:, :], half, 1)
    return jnp.where((column >= half) | (column > row), top, jnp.where(column < row, low, 0.0))


def unpack(packed):
    half, rows = packed.shape
    row, column = corner(rows)
    over = jnp.concatenate([packed, jnp.zeros_like(packed)], 0).T
    top = jnp.where((column >= half) | (column > row), packed, jnp.where(column < row, -over[:half, :], 0.0))
    moved, over_moved = pltpu.roll(packed, half, 1), pltpu.roll(over[:half, :], half, 1)
    low = jnp.where(column - half < row, moved, jnp.where(column - half > row, -over_moved, 0.0))
    return jnp.concatenate([top, jnp.where(column < half, -over[half:, :], low)], 0)


def lay_out(block, part, which, packed):
    rows, columns = part.shape
    if not packed:
        for j in range(columns // LANES):
            block[j * rows:(j + 1) * rows, :] = part[:, j * LANES:(j + 1) * LANES]
        return
    count = columns // rows
    for j in range(count - 1):
        at = jnp.where(j < which, j, j + 1)
        block[j * rows:(j + 1) * rows, :] = part[:, pl.ds(pl.multiple_of(at * rows, LANES), rows)]
    block[(count - 1) * rows:, :] = pack(part[:, pl.ds(pl.multiple_of(which * rows, LANES), rows)])


def sign(turned_level, weight):
    return weight[...] * (0.5 - bit(turned_level).astype(f32))


def first_block_kernel(turned_level, which_of, far, far_other, left, right_high, right_low, weight, half_way, block, full, columns):
    place(full, [far], [far_other])
    half_way[...] = product_of(split(full[...]), (right_high[...], right_low[...]))
    rows = columns.shape[0]
    which = which_of(lax.axis_index("ens"))
    at = pl.ds(pl.multiple_of(which * rows, LANES), rows)
    full[...] = product(left[...], half_way[...])
    columns[...] = sign(turned_level, weight) * (full[at, :] - full[:, at].T)
    lay_out(block, columns, which, True)


def blocks_kernel(turned_level, which_of, packed, half_way, left, weight, *refs):
    blocks, terms = refs[:-1], refs[-1]
    cyclic = product(left[...], half_way[...])
    terms[...] = sign(turned_level, weight) * (cyclic - cyclic.T)
    rows = terms.shape[0] // lax.axis_size("ens")
    here = lax.axis_index("ens")
    for which, block in zip(which_of(here), blocks):
        lay_out(block, terms.at[pl.ds(pl.multiple_of(which * rows, 8), rows), :], which, packed)


def skew_block(turned_level, which, half_way, left, weight, block, columns):
    rows = columns.shape[0]
    at = pl.ds(pl.multiple_of(which * rows, LANES), rows)
    across = product(left[...], half_way[:, at]).T
    columns[...] = sign(turned_level, weight) * (product(left[at, :], half_way[...]) - across)
    lay_out(block, columns, which, True)


def later_blocks_kernel(turned_level, which_of, half_way, left, weight, own, *refs):
    blocks_kernel(turned_level, which_of, True, half_way, left, weight, *refs[:-1])
    skew_block(turned_level, lax.axis_index("ens"), half_way, left, weight, own, refs[-1])


def half_way_kernel(far, far_other, right_high, right_low, half_way, full):
    place(full, [far], [far_other])
    half_way[...] = product_of(split(full[...]), (right_high[...], right_low[...]))


def sum_kernel(rows, packed, *refs):
    terms, (out, total) = refs[:-2], refs[-2:]
    spread = out.shape[0] // rows
    here = lax.axis_index("ens")
    added = terms[0][...]
    for term in terms[1:-1]:
        added = added + term[...]
    added = added + jnp.where((lax.axis_size("ens") != 4) | (here == 0) | (here == 3), terms[-1][...], 0.0)
    if packed:
        total[:(spread - 1) * rows, :] = added[:(spread - 1) * rows, :]
        total[(spread - 1) * rows:, :] = unpack(added[(spread - 1) * rows:, :])
    else:
        total[...] = added
    for j in range(spread):
        at = jnp.where(j < here, j, jnp.where(j == here, spread - 1, j - 1)) if packed else j
        out[pl.ds(j, rows, stride=spread), :] = total[pl.ds(pl.multiple_of(at * rows, 8), rows), :]


def send_rows(blocks):
    members = len(blocks)

    def move(x, pairs):
        return lax.ppermute(x, "ens", pairs)

    if members != 4:
        return [move(blocks[s], [(i, (i + s) % members) for i in range(members)]) for s in range(1, members)]
    _, beside, over_two, across = blocks
    over = move(over_two, [(0, 1), (1, 3), (3, 2), (2, 0)])
    arrived = [move(across, [(0, 3), (3, 0)]), move(beside, [(0, 1), (1, 0), (2, 3), (3, 2)])]
    return [*arrived, move(across + over, [(1, 2), (2, 1)]), over]


def shards(levels, members, propagators, weights, target):
    order = target.shape[0]
    square = (order, order)
    slices = 1 << levels
    count = len(PIECES)
    pieces = [(order // 2 * p // sum(PIECES), order) for p in PIECES]

    def swap(x, level):
        return lax.ppermute(x, "tm", [(i, i ^ (1 << level)) for i in range(slices)])

    slice_here = propagators[0, 0]
    other = swap(slice_here, 0)
    mine = call(early_kernel, [square], slice_here)[0]
    sends = call(send_kernel, pieces, mine, other)
    own, left, right = call(functools.partial(own_kernel, levels == 3), [square] * 3, mine, other, target)
    top = levels - 1
    for level in range(1, top):
        got = [swap(s, level) for s in sends]
        products = [call(half_kernel, [g.shape], g, own)[0] for g in got]
        if level + 1 < top:
            outs = call(
                functools.partial(turn_kernel, top, level, count), [square] * 3 + pieces, *products,
                *[swap(p, 0) for p in products], *got, *[swap(g, 0) for g in got], left, right, target, scratch=[square])
            (own, left, right), sends = outs[:3], outs[3:]
    far = [swap(p, top) for p in products]
    near = call(join_kernel, [(order // 2, order)], *got)[0]
    right = call(factor_kernel, [(square, bf16)] * 2, near, swap(near, 0), right, scratch=[square])
    far = call(join_kernel, [(order // 2, order)], *far)[0]
    rows, spread = order // members, order // LANES
    packed = rows == LANES
    block = (rows * spread - packed * rows // 2, LANES)
    factors = (far, swap(far, 0), left, *right, weights.reshape(1, 1))
    if members == 4 and packed:
        half_way, over_two = call(
            functools.partial(first_block_kernel, top - 1, lambda here: here ^ 2), [square, block], *factors,
            scratch=[square, (rows, order)])
        blocks = call(
            functools.partial(later_blocks_kernel, top - 1, lambda here: (here ^ 1, here ^ 3)), [block] * 3,
            half_way, left, factors[-1], scratch=[square, (rows, order)])
        blocks = [blocks[0], blocks[1], over_two, blocks[2]]
    else:
        order_of = (lambda here: [here ^ s for s in range(members)]) if members == 4 else (
            lambda here: [lax.rem(here + s, members) for s in range(members)])
        half_way = call(half_way_kernel, [square], *factors[:2], *right, scratch=[square])[0]
        blocks = call(
            functools.partial(blocks_kernel, top - 1, order_of, packed), [block] * members, half_way, left, factors[-1],
            scratch=[square])
    arrived = send_rows(blocks)
    total = call(
        functools.partial(sum_kernel, rows, packed), [(rows * spread, LANES)], blocks[0], *arrived,
        scratch=[(rows * spread, LANES)])[0]
    return total.reshape(rows, 1, order)


def solution(mesh):
    levels = mesh.shape["tm"].bit_length() - 1
    assert mesh.shape["tm"] == 1 << levels and levels >= 3
    placed = (P("ens", "tm", None, None), P("ens"), P())
    return jax.shard_map(
        functools.partial(shards, levels, mesh.shape["ens"]),
        mesh=mesh, in_specs=placed, out_specs=P("ens", "tm", None), check_vma=False)
```

```python
import functools

import jax
import jax.numpy as jnp
from jax import lax
from jax.experimental import pallas as pl
from jax.experimental.pallas import tpu as pltpu
from jax.sharding import PartitionSpec as P

LANES = 128
PIECES = (1, 1, 1, 1)
f32, bf16 = jnp.float32, jnp.bfloat16


def split(x):
    high = x.astype(bf16)
    return high, (x - high.astype(f32)).astype(bf16)


def product(a, b, b_turned=False):
    return product_of(split(a), split(b), b_turned)


def product_of(a, b, b_turned=False):
    (ah, al), (bh, bl) = a, b
    dims = (((1,), (1 if b_turned else 0,)), ((), ()))
    dot = functools.partial(lax.dot_general, dimension_numbers=dims, preferred_element_type=f32)
    return dot(ah, bh) + (dot(al, bh) + dot(ah, bl))


def bit(level):
    return lax.rem(lax.div(lax.axis_index("tm"), 1 << level), 2)


def call(kernel, outs, *operands, scratch=()):
    return pl.pallas_call(
        kernel,
        out_shape=[jax.ShapeDtypeStruct(s, f32) if isinstance(s[0], int) else jax.ShapeDtypeStruct(*s) for s in outs],
        in_specs=[pl.BlockSpec(memory_space=pltpu.VMEM)] * len(operands),
        out_specs=[pl.BlockSpec(memory_space=pltpu.VMEM)] * len(outs),
        scratch_shapes=[pltpu.VMEM(s, f32) for s in scratch],
        compiler_params=pltpu.CompilerParams(vmem_limit_bytes=16 << 20),
    )(*operands)


def place(full, mine, other):
    half = full.shape[0] // 2
    core = bit(0)
    for pieces, base in ((mine, core * half), (other, (1 - core) * half)):
        at = 0
        for piece in pieces:
            rows = piece.shape[0]
            full[pl.ds(pl.multiple_of(base + at, 8), rows), :] = piece[...]
            at += rows


def cut(rows, pieces):
    at = 0
    for piece in pieces:
        piece[...] = rows[at:at + piece.shape[0], :]
        at += piece.shape[0]


def early_kernel(slice_here, mine):
    mine[...] = slice_here[...]


def send_kernel(mine, other, *sends):
    core, turned = bit(0), bit(1)
    half = mine.shape[0] // 2

    @pl.when((turned == 0) & (core == 0))
    def _():
        cut(product(other[...], mine[:, :half]).T, sends)

    @pl.when((turned == 0) & (core == 1))
    def _():
        cut(product(mine[...], other[:, half:]).T, sends)

    @pl.when((turned == 1) & (core == 0))
    def _():
        cut(product(other[:half, :], mine[...]), sends)

    @pl.when((turned == 1) & (core == 1))
    def _():
        cut(product(mine[half:, :], other[...]), sends)


def own_kernel(short, mine, other, target, own, left, right):
    core, turned = bit(0), bit(1)
    takes = (bit(2) == turned) if short else (core < 0)

    def identity(out):
        row, column = (lax.broadcasted_iota(jnp.int32, out.shape, d) for d in (0, 1))
        out[...] = (row == column).astype(f32)

    @pl.when((core == 0) & (turned == 0))
    def _():
        left[...] = mine[...]
        right[...] = other[...]

        @pl.when(takes)
        def _():
            left[...] = product(left[...], target[...], b_turned=True)

        own[...] = product(other[...], left[...])

    @pl.when((core == 0) & (turned == 1))
    def _():
        left[...] = other[...].T
        right[...] = mine[...].T

        @pl.when(takes)
        def _():
            left[...] = product(left[...], target[...])

        own[...] = product(right[...], left[...])

    @pl.when((core == 1) & (turned == 0))
    def _():
        own[...] = product(mine[...], other[...])
        identity(right)

        @pl.when(takes)
        def _():
            own[...] = product(own[...], target[...], b_turned=True)

        left[...] = own[...]

    @pl.when((core == 1) & (turned == 1))
    def _():
        right[...] = product(mine[...], other[...]).T
        own[...] = right[...]
        identity(left)

        @pl.when(takes)
        def _():
            left[...] = target[...]
            own[...] = product(right[...], target[...])


def turn_kernel(top, level, count, *refs):
    mine, other, got, got_other = (refs[i * count:(i + 1) * count] for i in range(4))
    left, right, target, own, left_out, right_out = refs[4 * count:4 * count + 6]
    sends, full = refs[4 * count + 6:-1], refs[-1]
    half = full.shape[0] // 2
    flip = bit(level) != bit(level + 1)
    place(full, got, got_other)
    new_right = product(full[...], right[...])
    place(full, mine, other)

    @pl.when(flip)
    def _():
        own[...] = full[...].T
        left_out[...] = new_right.T
        right_out[...] = left[...].T

    @pl.when(jnp.logical_not(flip))
    def _():
        own[...] = full[...]
        full[...] = full[...].T
        left_out[...] = left[...]
        right_out[...] = new_right

    cut(full[pl.ds(pl.multiple_of(bit(0) * half, 8), half), :], sends)
    if level + 2 == top:
        for out in own, left_out:
            @pl.when((bit(top) == bit(level + 1)) & (bit(top) == 0))
            def _(out=out):
                out[...] = product(out[...], target[...], b_turned=True)

            @pl.when((bit(top) == bit(level + 1)) & (bit(top) == 1))
            def _(out=out):
                out[...] = product(out[...], target[...])


def half_kernel(got, own, out):
    out[...] = product(got[...], own[...])


def join_kernel(*refs):
    at = 0
    for piece in refs[:-1]:
        refs[-1][at:at + piece.shape[0], :] = piece[...]
        at += piece.shape[0]


def near_kernel(*refs):
    left, joined, high, low = refs[-4:]
    join_kernel(*refs[:-4], joined)
    high[...], low[...] = split(left[...])


def factor_kernel(near, near_other, right, high, low, full):
    place(full, [near], [near_other])
    high[...], low[...] = split(product(full[...], right[...]))


def corner(rows):
    return [lax.broadcasted_iota(jnp.int32, (rows // 2, rows), d) for d in (0, 1)]


def pack(square):
    rows = square.shape[0]
    half = rows // 2
    row, column = corner(rows)
    top, low = square[:half, :], pltpu.roll(square[half:, :], half, 1)
    return jnp.where((column >= half) | (column > row), top, jnp.where(column < row, low, 0.0))


def unpack(packed):
    half, rows = packed.shape
    row, column = corner(rows)
    over = jnp.concatenate([packed, jnp.zeros_like(packed)], 0).T
    top = jnp.where((column >= half) | (column > row), packed, jnp.where(column < row, -over[:half, :], 0.0))
    moved, over_moved = pltpu.roll(packed, half, 1), pltpu.roll(over[:half, :], half, 1)
    low = jnp.where(column - half < row, moved, jnp.where(column - half > row, -over_moved, 0.0))
    return jnp.concatenate([top, jnp.where(column < half, -over[half:, :], low)], 0)


def lay_out(block, part, which, packed):
    rows, columns = part.shape
    if not packed:
        for j in range(columns // LANES):
            block[j * rows:(j + 1) * rows, :] = part[:, j * LANES:(j + 1) * LANES]
        return
    count = columns // rows
    for j in range(count - 1):
        at = jnp.where(j < which, j, j + 1)
        block[j * rows:(j + 1) * rows, :] = part[:, pl.ds(pl.multiple_of(at * rows, LANES), rows)]
    block[(count - 1) * rows:, :] = pack(part[:, pl.ds(pl.multiple_of(which * rows, LANES), rows)])


def sign(turned_level, weight):
    return weight[...] * (0.5 - bit(turned_level).astype(f32))


def first_block_kernel(turned_level, which_of, far, far_other, left_high, left_low, right_high, right_low, weight, half_way, block, full, columns):
    place(full, [far], [far_other])
    half_way[...] = product_of(split(full[...]), (right_high[...], right_low[...]))
    rows = columns.shape[0]
    which = which_of(lax.axis_index("ens"))
    at = pl.ds(pl.multiple_of(which * rows, LANES), rows)
    full[...] = product_of((left_high[...], left_low[...]), split(half_way[...]))
    columns[...] = sign(turned_level, weight) * (full[at, :] - full[:, at].T)
    lay_out(block, columns, which, True)


def blocks_kernel(turned_level, which_of, packed, half_way, left, weight, *refs):
    blocks, terms = refs[:-1], refs[-1]
    cyclic = product(left[...], half_way[...])
    terms[...] = sign(turned_level, weight) * (cyclic - cyclic.T)
    rows = terms.shape[0] // lax.axis_size("ens")
    here = lax.axis_index("ens")
    for which, block in zip(which_of(here), blocks):
        lay_out(block, terms.at[pl.ds(pl.multiple_of(which * rows, 8), rows), :], which, packed)


def skew_block(turned_level, which, half_way, left, weight, block, columns):
    rows = columns.shape[0]
    at = pl.ds(pl.multiple_of(which * rows, LANES), rows)
    across = product(left[...], half_way[:, at]).T
    columns[...] = sign(turned_level, weight) * (product(left[at, :], half_way[...]) - across)
    lay_out(block, columns, which, True)


def later_blocks_kernel(turned_level, which_of, half_way, left, weight, own, *refs):
    blocks_kernel(turned_level, which_of, True, half_way, left, weight, *refs[:-1])
    skew_block(turned_level, lax.axis_index("ens"), half_way, left, weight, own, refs[-1])


def half_way_kernel(far, far_other, right_high, right_low, half_way, full):
    place(full, [far], [far_other])
    half_way[...] = product_of(split(full[...]), (right_high[...], right_low[...]))


def sum_kernel(rows, packed, *refs):
    terms, (out, total) = refs[:-2], refs[-2:]
    spread = out.shape[0] // rows
    here = lax.axis_index("ens")
    added = terms[0][...]
    for term in terms[1:-1]:
        added = added + term[...]
    added = added + jnp.where((lax.axis_size("ens") != 4) | (here == 0) | (here == 3), terms[-1][...], 0.0)
    if packed:
        total[:(spread - 1) * rows, :] = added[:(spread - 1) * rows, :]
        total[(spread - 1) * rows:, :] = unpack(added[(spread - 1) * rows:, :])
    else:
        total[...] = added
    for j in range(spread):
        at = jnp.where(j < here, j, jnp.where(j == here, spread - 1, j - 1)) if packed else j
        out[pl.ds(j, rows, stride=spread), :] = total[pl.ds(pl.multiple_of(at * rows, 8), rows), :]


def send_rows(blocks):
    members = len(blocks)

    def move(x, pairs):
        return lax.ppermute(x, "ens", pairs)

    if members != 4:
        return [move(blocks[s], [(i, (i + s) % members) for i in range(members)]) for s in range(1, members)]
    _, beside, over_two, across = blocks
    over = move(over_two, [(0, 1), (1, 3), (3, 2), (2, 0)])
    arrived = [move(across, [(0, 3), (3, 0)]), move(beside, [(0, 1), (1, 0), (2, 3), (3, 2)])]
    return [*arrived, move(across + over, [(1, 2), (2, 1)]), over]


def shards(levels, members, propagators, weights, target):
    order = target.shape[0]
    square = (order, order)
    slices = 1 << levels
    count = len(PIECES)
    pieces = [(order // 2 * p // sum(PIECES), order) for p in PIECES]

    def swap(x, level):
        return lax.ppermute(x, "tm", [(i, i ^ (1 << level)) for i in range(slices)])

    slice_here = propagators[0, 0]
    other = swap(slice_here, 0)
    mine = call(early_kernel, [square], slice_here)[0]
    sends = call(send_kernel, pieces, mine, other)
    own, left, right = call(functools.partial(own_kernel, levels == 3), [square] * 3, mine, other, target)
    top = levels - 1
    for level in range(1, top):
        got = [swap(s, level) for s in sends]
        products = [call(half_kernel, [g.shape], g, own)[0] for g in got]
        if level + 1 < top:
            outs = call(
                functools.partial(turn_kernel, top, level, count), [square] * 3 + pieces, *products,
                *[swap(p, 0) for p in products], *got, *[swap(g, 0) for g in got], left, right, target, scratch=[square])
            (own, left, right), sends = outs[:3], outs[3:]
    far = [swap(p, top) for p in products]
    near, *left_parts = call(near_kernel, [(order // 2, order)] + [(square, bf16)] * 2, *got, left)
    right = call(factor_kernel, [(square, bf16)] * 2, near, swap(near, 0), right, scratch=[square])
    far = call(join_kernel, [(order // 2, order)], *far)[0]
    rows, spread = order // members, order // LANES
    packed = rows == LANES
    block = (rows * spread - packed * rows // 2, LANES)
    factors = (far, swap(far, 0), *left_parts, *right, weights.reshape(1, 1))
    if members == 4 and packed:
        half_way, over_two = call(
            functools.partial(first_block_kernel, top - 1, lambda here: here ^ 2), [square, block], *factors,
            scratch=[square, (rows, order)])
        blocks = call(
            functools.partial(later_blocks_kernel, top - 1, lambda here: (here ^ 1, here ^ 3)), [block] * 3,
            half_way, left, factors[-1], scratch=[square, (rows, order)])
        blocks = [blocks[0], blocks[1], over_two, blocks[2]]
    else:
        order_of = (lambda here: [here ^ s for s in range(members)]) if members == 4 else (
            lambda here: [lax.rem(here + s, members) for s in range(members)])
        half_way = call(half_way_kernel, [square], *factors[:2], *right, scratch=[square])[0]
        blocks = call(
            functools.partial(blocks_kernel, top - 1, order_of, packed), [block] * members, half_way, left, factors[-1],
            scratch=[square])
    arrived = send_rows(blocks)
    total = call(
        functools.partial(sum_kernel, rows, packed), [(rows * spread, LANES)], blocks[0], *arrived,
        scratch=[(rows * spread, LANES)])[0]
    return total.reshape(rows, 1, order)


def solution(mesh):
    levels = mesh.shape["tm"].bit_length() - 1
    assert mesh.shape["tm"] == 1 << levels and levels >= 3
    placed = (P("ens", "tm", None, None), P("ens"), P())
    return jax.shard_map(
        functools.partial(shards, levels, mesh.shape["ens"]),
        mesh=mesh, in_specs=placed, out_specs=P("ens", "tm", None), check_vma=False)
```
